32 devices in a mesh: group: 4 (over x, core), tp: 8 (over z, y).
Axes of the slice: x: 2, y: 2, z: 4, core: 2. Of those that a mesh axis runs over, the one named last changes fastest.
Arguments:
- hidden: bfloat16 [4096, 28672], P('group', 'tp'), may hold values from -6 to 6
- residual: bfloat16 [4096, 8192], P('group', 'tp'), may hold values from -6 to 6
- down_projection_weight: bfloat16 [28672, 8192], P('tp'), may hold values from -0.03125 to 0.03125
- adapter_down_maps: bfloat16 [128, 64, 28672], P('group', None, 'tp'), may hold values from -0.03125 to 0.03125
- adapter_up_maps: bfloat16 [128, 64, 8192], P('group', None, 'tp'), may hold values from -0.75 to 0.75
- row_adapter_index: int32 [4096, 1], P('group'), may hold values from 0 to 127; in each aligned block of 1024 rows (0 to 1023, 1024 to 2047, ...) at most 16 rows name the same one
Outputs:
- layer_out: bfloat16 [4096, 8192], P('group', 'tp')
The draws below stay inside these ranges and needn't reach their ends.
Inputs may be any that keep to these rules, and one draw needn't show every extreme that they name: `row_adapter_index`: within the 1024 rows of one group no adapter is named by more than 16 rows; in some group some adapter is named by exactly 16 rows; every adapter is named by some row.
All inputs are finite; a program needn't handle non-finite values.
Results may differ from the reference program's by a relative error of at most 0.02.
Values may be sent and summed in bfloat16 or wider, within the bound.
A program may use at most 256 MiB of HBM per device.

```python
import math
import jax
import jax.numpy as jnp
import numpy as np
from jax import lax

MODEL_WIDTH = 8192
HIDDEN_UNITS = 28672
ADAPTER_RANK = 64
MOST = 16
ROWS_G = 1024
ROWS = 4096
ADAPTER_COUNT = 128
N_TP = 8


def levels(stream_key, shape, cuts, least, top_value):
    def one(dim, parts):
        heights = jax.random.uniform(jax.random.fold_in(jax.random.fold_in(stream_key, 6), dim), (parts,), jnp.float32, least / len(cuts), top_value / len(cuts))
        return jnp.repeat(jnp.exp(heights), shape[dim] // parts).reshape((-1,) + (1,) * (len(shape) - dim - 1))

    gain = one(*cuts[0])
    for cut in cuts[1:]:
        gain = gain * one(*cut)
    return gain


def shared_out(stream_key, own, number, rows, number_of, top, most, slope):
    order = jax.random.permutation(stream_key, number_of)
    crowded, ordinary = portions_of(number_of, rows * top, most, slope, True), portions_of(number_of, rows * top, most, slope, False)
    places = jnp.arange(number_of)

    def named(tallies, turn):
        used = int((tallies > 0).sum())
        fixed = max(1, used // 4)
        moved = fixed + (places - fixed + turn * (used - fixed)) % max(1, number_of - fixed)
        return jnp.zeros((number_of,), jnp.int32).at[order[jnp.where(places < fixed, places, moved)]].set(jnp.asarray(tallies, jnp.int32))

    tallies = jnp.where(number % 4 == 0, named(crowded, number // 4), named(ordinary, number - number // 4 - 1))
    mixed = jax.random.permutation(jax.random.fold_in(own, 3), number_of)
    source_of, taker = mixed[0:number_of // 2 * 2:2], mixed[1:number_of // 2 * 2:2]
    room = jnp.minimum(tallies[source_of] - 1, most - tallies[taker]) // 2
    room = jnp.where((source_of == order[0]) | (taker == order[0]) | (tallies[taker] == 0), 0, jnp.maximum(room, 0))
    moved = jax.random.randint(jax.random.fold_in(own, 4), (number_of // 2,), 0, 1 << 20) % (room + 1)
    tallies = tallies.at[source_of].add(-moved).at[taker].add(moved)
    items = jnp.searchsorted(jnp.cumsum(tallies), jnp.arange(rows * top), side="right").astype(jnp.int32)
    listing = items.reshape(top, rows).T
    listing = listing[jax.random.permutation(jax.random.fold_in(own, 1), rows)]
    turn = jax.random.randint(jax.random.fold_in(own, 2), (rows, 1), 0, top)
    return jnp.take_along_axis(listing, (jnp.arange(top)[None, :] + turn) % top, axis=1)


def portions_of(count, total, reach, slope, full):
    loads = [(1 << 20) // math.isqrt(grade ** slope) + 1 for grade in range(1, count + 1)]
    largest = reach if full else min(reach, max(-(-total // count), total * loads[0] // sum(loads)))
    least = 1 if total - largest >= count - 1 else 0
    holding, spare = [largest] + [least] * (count - 1), total - largest - least * (count - 1)
    while spare > 0:
        candidates = [i for i in range(1, count) if holding[i] < largest] or [i for i in range(1, count) if holding[i] < reach]
        mass, left = sum([loads[i] for i in candidates]), spare
        for i in candidates:
            more = min(reach - holding[i], max(1, left * loads[i] // mass), spare)
            holding[i] = holding[i] + more
            spare = spare - more
    return np.array(holding)


def noise(key, dims, scale, most, pieces=(), kind=jnp.bfloat16):
    drawn = scale * jax.random.normal(key, dims, jnp.float32)
    if pieces:
        drawn = drawn * levels(key, dims, pieces, -0.22, 0.18)
    return jnp.clip(drawn, -most, most).astype(kind)


def setup_inputs(seed: int = 0) -> dict:
    streams_of = jax.random.split(jax.random.key(seed), 7)
    hidden = noise(streams_of[0], (ROWS, HIDDEN_UNITS), 1.0, 6.0, ((0, 4), (1, 8)))
    residual = noise(streams_of[1], (ROWS, MODEL_WIDTH), 1.0, 6.0, ((0, 4), (1, 8)))
    down_projection_weight = noise(streams_of[2], (HIDDEN_UNITS, MODEL_WIDTH), HIDDEN_UNITS ** -0.5, 0.03125, ((0, 8),))
    adapter_down_maps = noise(streams_of[3], (ADAPTER_COUNT, ADAPTER_RANK, HIDDEN_UNITS), HIDDEN_UNITS ** -0.5, 0.03125, ((0, 4), (2, 8)))
    adapter_up_maps = noise(streams_of[4], (ADAPTER_COUNT, ADAPTER_RANK, MODEL_WIDTH), ADAPTER_RANK ** -0.5, 0.75, ((0, 4), (2, 8)))
    row_adapter_index_keys = jax.random.split(jax.random.fold_in(streams_of[5], 1), ROWS // ROWS_G)
    row_adapter_index_turns = jax.random.permutation(jax.random.fold_in(streams_of[5], 3), ROWS // ROWS_G)
    row_adapter_index = jax.vmap(lambda own, number: shared_out(jax.random.fold_in(streams_of[5], 2), own, number, ROWS_G, ADAPTER_COUNT, 1, MOST, 2))(row_adapter_index_keys, row_adapter_index_turns).reshape((ROWS, 1))
    return dict(hidden=hidden, residual=residual, down_projection_weight=down_projection_weight, adapter_down_maps=adapter_down_maps, adapter_up_maps=adapter_up_maps, row_adapter_index=row_adapter_index)


def reference(hidden, residual, down_projection_weight, adapter_down_maps, adapter_up_maps, row_adapter_index):
    piece = HIDDEN_UNITS // N_TP

    def add_piece(total, index):
        start = index * piece
        part_hidden = lax.dynamic_slice_in_dim(hidden, start, piece, 1)
        part_weight = lax.dynamic_slice_in_dim(down_projection_weight, start, piece, 0)
        term = jnp.dot(part_hidden, part_weight, preferred_element_type=jnp.float32).astype(jnp.bfloat16)
        term = lax.optimization_barrier(term)
        return total + term.astype(jnp.float32), None

    base, _ = lax.scan(add_piece, jnp.zeros((ROWS, MODEL_WIDTH), jnp.float32), jnp.arange(N_TP, dtype=jnp.int32))

    def one_row(item):
        decode_row_vector, adapter_index = item
        rank_mixture = jnp.dot(adapter_down_maps[adapter_index], decode_row_vector, preferred_element_type=jnp.float32).astype(jnp.bfloat16)
        return jnp.dot(rank_mixture, adapter_up_maps[adapter_index], preferred_element_type=jnp.float32).astype(jnp.bfloat16)

    delta = lax.map(one_row, (hidden, row_adapter_index[:, 0]))
    total = residual.astype(jnp.float32) + base + delta.astype(jnp.float32)
    return total.astype(jnp.bfloat16)
```

```python
import functools

import jax
import jax.numpy as jnp
from jax import lax
from jax.experimental import pallas as pl
from jax.experimental.pallas import tpu as pltpu
from jax.sharding import PartitionSpec as P

MESH = pl.DeviceIdType.MESH
F32 = jnp.float32
BF16 = jnp.bfloat16
X_PARTS = 4


def kernel(
    n, groups, rank, tile,
    idr, idc, hid, res, w, a, b,
    out, xh, asib, bsib,
    hv, wv, pv, ring, av, xv, acc, ev, rv, dsend, drecv, mixb, rs, ag,
    ring_send, ring_recv, w_sem, a_sem, x_send, x_recv, sib_send, sib_recv,
    rs_send, rs_recv, ag_send, ag_recv, d_send, d_recv, loc, out_sem,
):
    rows, depth = hid.shape
    feats = res.shape[1]
    half = feats // 2
    a_rows = a.shape[0]
    tiles = a_rows // tile
    per_tile = tile // rank
    residents = a_rows // rank
    part = rows // X_PARTS
    sub = rows // 2
    block = 2 * rows // n
    blocks = n // 2

    t, g = lax.axis_index("tp"), lax.axis_index("group")
    z, y = t // 2, lax.rem(t, 2)
    pos = z + y * (n - 1 - 2 * z)

    def at(p):
        p = lax.rem(p + 2 * n, n)
        c = p // (n // 2)
        return 2 * p * (1 - c) + c * (2 * (n - 1 - p) + 1)

    toward = (at(pos + 1), at(pos - 1))
    across = lax.rem(g + groups // 2, groups)
    sibling = g + 1 - 2 * lax.rem(g, 2)

    barrier = pltpu.get_barrier_semaphore()
    for k in range(1, n):
        pl.semaphore_signal(
            barrier, inc=1, device_id=(g, lax.rem(t + k, n)), device_id_type=MESH
        )
    for other in (across, sibling):
        pl.semaphore_signal(barrier, inc=1, device_id=(other, t), device_id_type=MESH)

    own_copy = pltpu.make_async_copy(hid, hv, loc.at[0])
    own_copy.start()

    def w_copy(s, d):
        hops = n - 1 - s
        dest = at(pos + hops) if d == 0 else at(pos - hops)
        column = pl.multiple_of(dest * feats + d * half, half)
        return pltpu.make_async_copy(
            w.at[:, pl.ds(column, half)], wv.at[d, pl.ds(0, depth)], w_sem.at[d]
        )

    for d in range(2):
        w_copy(0, d).start()
    res_copy = pltpu.make_async_copy(res, rv, loc.at[1])
    res_copy.start()
    pl.semaphore_wait(barrier, n + 1)

    def x_copy(c):
        where = pl.ds(pl.multiple_of(c * part, part), part)
        return pltpu.make_async_remote_copy(
            src_ref=hid.at[where], dst_ref=xh.at[where],
            send_sem=x_send.at[c], recv_sem=x_recv.at[c],
            device_id=(across, t), device_id_type=MESH,
        )

    a_copy = pltpu.make_async_remote_copy(
        src_ref=a, dst_ref=asib, send_sem=sib_send.at[0], recv_sem=sib_recv.at[0],
        device_id=(sibling, t), device_id_type=MESH,
    )
    b_copy = pltpu.make_async_remote_copy(
        src_ref=b, dst_ref=bsib, send_sem=sib_send.at[1], recv_sem=sib_recv.at[1],
        device_id=(sibling, t), device_id_type=MESH,
    )
    x_copy(0).start()
    x_copy(1).start()
    a_copy.start()
    b_copy.start()
    acc[...] = jnp.zeros_like(acc)
    own_copy.wait()

    def partial(s, d):
        w_copy(s, d).wait()
        width = min(256, half)

        def columns(i, carry):
            where = pl.ds(pl.multiple_of(i * width, width), width)
            pv[d, :, where] = jnp.dot(
                hv[...], wv[d, pl.ds(0, depth), where], preferred_element_type=F32
            )
            return carry

        lax.fori_loop(0, half // width, columns, 0)

        @pl.when(s + 1 < n)
        def _():
            w_copy(s + 1, d).start()

    def adapter_of(i):
        theirs = i // tiles
        owner = g * (1 - theirs) + sibling * theirs
        return owner * residents + lax.rem(i, tiles) * per_tile

    def a_start(i, slot):
        @pl.when(i < tiles)
        def _():
            where = pl.ds(pl.multiple_of(lax.rem(i, tiles) * tile, tile), tile)
            pltpu.make_async_copy(a.at[where], av.at[slot], a_sem.at[slot]).start()

        @pl.when(i >= tiles)
        def _():
            where = pl.ds(pl.multiple_of(lax.rem(i, tiles) * tile, tile), tile)
            pltpu.make_async_copy(asib.at[where], av.at[slot], a_sem.at[slot]).start()

    def mix(first, count, rows_ref, column, width, ids_row):
        a_start(first, 0)

        def one(i, carry):
            @pl.when(i + 1 < count)
            def _():
                a_start(first + i + 1, lax.rem(i + 1, 2))

            slot = lax.rem(i, 2)
            pltpu.make_async_copy(
                a.at[pl.ds(0, tile)], av.at[slot], a_sem.at[slot]
            ).wait()
            products = lax.dot_general(
                av[slot], rows_ref[...], (((1,), (1,)), ((), ())),
                preferred_element_type=F32,
            )
            start = adapter_of(first + i)
            ids = idr[pl.ds(ids_row, 1), pl.ds(column, width)]
            where = pl.ds(pl.multiple_of(ids_row * rows + column, width), width)
            total = acc[:, where]
            for j in range(per_tile):
                total = total + jnp.where(
                    ids == start + j, products[j * rank:(j + 1) * rank], 0.0
                )
            acc[:, where] = total
            return carry

        lax.fori_loop(0, count, one, 0)

    def mix_across(c):
        x_copy(c).wait_recv()
        where = pl.ds(pl.multiple_of(c * part, part), part)
        copy = pltpu.make_async_copy(xh.at[where], xv, loc.at[2])
        copy.start()
        copy.wait()
        mix(0, 2 * tiles, xv, pl.multiple_of(c * part, part), part, 1)

    def ring_copy(s, d, h):
        where = pl.ds(h * sub, sub)
        return pltpu.make_async_remote_copy(
            src_ref=ring.at[d, s, where], dst_ref=ring.at[d, s + 1, where],
            send_sem=ring_send.at[d, s, h], recv_sem=ring_recv.at[d, s + 1, h],
            device_id=(g, toward[d]), device_id_type=MESH,
        )

    per_turn = 2 * tiles // X_PARTS

    def step(s, carry):
        for d in range(2):
            partial(s, d)

            @pl.when(s == 0)
            def _():
                for h in range(2):
                    where = pl.ds(h * sub, sub)
                    ring[d, 0, where] = pv[d, where].astype(BF16)
                    ring_copy(s, d, h).start()

        turn = s // 2

        @pl.when((lax.rem(s, 2) == 1) & (turn < X_PARTS))
        def _():
            mix(turn * per_turn, per_turn, hv, 0, rows, 0)

        @pl.when((lax.rem(s, 2) == 0) & (turn >= 1) & (turn < X_PARTS))
        def _():
            @pl.when(turn == 1)
            def _():
                a_copy.wait_recv()

            mix_across(turn - 1)

            @pl.when(turn + 1 < X_PARTS)
            def _():
                x_copy(turn + 1).start()

        @pl.when(s > 0)
        def _():
            for h in range(2):
                where = pl.ds(h * sub, sub)
                for d in range(2):
                    ring_copy(s - 1, d, h).wait_recv()

                    @pl.when(s < n - 1)
                    def _():
                        ring[d, s, where] = (
                            ring[d, s, where].astype(F32) + pv[d, where]
                        ).astype(BF16)
                        ring_copy(s, d, h).start()

                    @pl.when(s == n - 1)
                    def _():
                        pv[d, where] = ring[d, s, where].astype(F32) + pv[d, where]

        return carry

    lax.fori_loop(0, n, step, 0)

    b_copy.wait_recv()
    b_copies = []
    for d in range(2):
        for i, source in enumerate((b, bsib)):
            b_copies.append(
                pltpu.make_async_copy(
                    source.at[:, pl.ds(d * half, half)],
                    wv.at[d, pl.ds(i * a_rows, a_rows)],
                    loc.at[3 + 2 * d + i],
                )
            )
    for copy in b_copies:
        copy.start()
    mix_across(X_PARTS - 1)

    for q in range(n):
        mixb[q] = acc[:, q * block:(q + 1) * block].astype(BF16)

    def slice_out(q):
        return pltpu.make_async_remote_copy(
            src_ref=mixb.at[q], dst_ref=rs.at[t],
            send_sem=rs_send.at[q], recv_sem=rs_recv.at[t],
            device_id=(g, q), device_id_type=MESH,
        )

    def slice_in(q):
        return pltpu.make_async_copy(mixb.at[q], rs.at[q], rs_recv.at[q])

    def sum_out(q):
        return pltpu.make_async_remote_copy(
            src_ref=ag.at[t], dst_ref=ag.at[t],
            send_sem=ag_send.at[q], recv_sem=ag_recv.at[t],
            device_id=(g, q), device_id_type=MESH,
        )

    def sum_in(q):
        return pltpu.make_async_copy(mixb.at[q], ag.at[q], ag_recv.at[q])

    for k in range(1, n):
        slice_out(lax.rem(t + k, n)).start()
    total = mixb[t].astype(F32)
    for k in range(1, n):
        q = lax.rem(t + k, n)
        slice_in(q).wait()
        total = total + rs[q].astype(F32)
    ag[t] = total.astype(BF16)
    for k in range(1, n):
        sum_out(lax.rem(t + k, n)).start()
    for k in range(1, n):
        sum_in(lax.rem(t + k, n)).wait()
    for copy in b_copies:
        copy.wait()

    def delta(q, d_write):
        mixes = ag[q].astype(F32)
        wide = jnp.concatenate([mixes] * per_tile, axis=0).T.astype(BF16)
        ids = idc[pl.ds(pl.multiple_of(q * block, block), block), :]
        lane = lax.broadcasted_iota(jnp.int32, (block, tile), 1) // rank
        for i in range(2 * tiles):
            owner = g if i < tiles else sibling
            start = owner * residents + (i % tiles) * per_tile
            ev[:, i * tile:(i + 1) * tile] = jnp.where(
                ids == start + lane, wide, jnp.zeros_like(wide)
            )
        for d in range(2):
            d_write(
                d,
                jnp.dot(
                    ev[...], wv[d, pl.ds(0, 2 * a_rows)], preferred_element_type=F32
                ).astype(BF16),
            )

    def delta_copy(j):
        return pltpu.make_async_remote_copy(
            src_ref=dsend.at[j], dst_ref=drecv.at[j],
            send_sem=d_send.at[j], recv_sem=d_recv.at[j],
            device_id=(across, t), device_id_type=MESH,
        )

    def across_block(j, carry):
        def write(d, value):
            dsend[j, :, d * half:(d + 1) * half] = value

        delta(blocks + j, write)
        delta_copy(j).start()
        return carry

    lax.fori_loop(0, blocks, across_block, 0)
    res_copy.wait()

    def own_block(j, carry):
        where = pl.ds(pl.multiple_of(j * block, block), block)

        def write(d, value):
            pv[d, where] = pv[d, where] + value.astype(F32)

        delta(j, write)
        return carry

    lax.fori_loop(0, blocks, own_block, 0)

    def out_copy(j):
        where = pl.ds(pl.multiple_of(j * block, block), block)
        return pltpu.make_async_copy(rv.at[where], out.at[where], out_sem.at[j])

    def finish(j, carry):
        where = pl.ds(pl.multiple_of(j * block, block), block)
        delta_copy(j).wait_recv()
        for d in range(2):
            columns = slice(d * half, (d + 1) * half)
            rv[where, columns] = (
                rv[where, columns].astype(F32)
                + (pv[d, where] + drecv[j, :, columns].astype(F32))
            ).astype(BF16)
        out_copy(j).start()
        return carry

    lax.fori_loop(0, blocks, finish, 0)

    def drain(s, carry):
        for d in range(2):
            for h in range(2):
                ring_copy(s, d, h).wait_send()
        return carry

    lax.fori_loop(0, n - 1, drain, 0)
    for c in range(X_PARTS):
        x_copy(c).wait_send()
    a_copy.wait_send()
    b_copy.wait_send()
    for k in range(1, n):
        q = lax.rem(t + k, n)
        slice_out(q).wait_send()
        sum_out(q).wait_send()
    for j in range(blocks):
        delta_copy(j).wait_send()
        out_copy(j).wait()


def per_device(
    hidden, residual, down_projection_weight, adapter_down_maps, adapter_up_maps, row_adapter_index
):
    n, groups = lax.axis_size("tp"), lax.axis_size("group")
    rows, depth = hidden.shape
    feats = residual.shape[1]
    half = feats // 2
    residents, rank, _ = adapter_down_maps.shape
    a_rows = residents * rank
    tile = 4 * rank
    block, blocks = 2 * rows // n, n // 2
    ids = row_adapter_index[:, 0]
    swap = [(i, (i + groups // 2) % groups) for i in range(groups)]
    both = jnp.stack([ids, lax.ppermute(ids, "group", swap)])
    hbm = pl.BlockSpec(memory_space=pl.ANY)
    vmem = pl.BlockSpec(memory_space=pltpu.VMEM)
    dma = pltpu.SemaphoreType.DMA
    bf16 = functools.partial(jax.ShapeDtypeStruct, dtype=BF16)
    outs = pl.pallas_call(
        functools.partial(kernel, n, groups, rank, tile),
        out_shape=[
            bf16((rows, feats)), bf16((rows, depth)),
            bf16((a_rows, depth)), bf16((a_rows, feats)),
        ],
        in_specs=[vmem, vmem, hbm, hbm, hbm, hbm, hbm],
        out_specs=[hbm] * 4,
        scratch_shapes=[
            pltpu.VMEM((rows, depth), BF16),
            pltpu.VMEM((2, max(depth, 2 * a_rows), half), BF16),
            pltpu.VMEM((2, rows, half), F32),
            pltpu.VMEM((2, n, rows, half), BF16),
            pltpu.VMEM((2, tile, depth), BF16),
            pltpu.VMEM((rows // X_PARTS, depth), BF16),
            pltpu.VMEM((rank, 2 * rows), F32),
            pltpu.VMEM((block, 2 * a_rows), BF16),
            pltpu.VMEM((rows, feats), BF16),
            pltpu.VMEM((blocks, block, feats), BF16),
            pltpu.VMEM((blocks, block, feats), BF16),
            pltpu.VMEM((n, rank, block), BF16),
            pltpu.VMEM((n, rank, block), BF16),
            pltpu.VMEM((n, rank, block), BF16),
            dma((2, n, 2)), dma((2, n, 2)), dma((2,)), dma((2,)),
            dma((X_PARTS,)), dma((X_PARTS,)), dma((2,)), dma((2,)),
            dma((n,)), dma((n,)), dma((n,)), dma((n,)),
            dma((blocks,)), dma((blocks,)), dma((7,)), dma((blocks,)),
        ],
        compiler_params=pltpu.CompilerParams(
            collective_id=0, has_side_effects=True, vmem_limit_bytes=62 * 2**20
        ),
        cost_estimate=pl.CostEstimate(
            flops=2 * rows * depth * (n * feats + 4 * a_rows),
            bytes_accessed=2 * depth * n * feats,
            transcendentals=0,
        ),
        name="ring_and_adapters",
    )(
        both, both.reshape(2 * rows, 1), hidden, residual, down_projection_weight,
        adapter_down_maps.reshape(a_rows, depth), adapter_up_maps.reshape(a_rows, feats),
    )
    return outs[0]


def solution(mesh):
    in_specs = (
        P("group", "tp"),
        P("group", "tp"),
        P("tp", None),
        P("group", None, "tp"),
        P("group", None, "tp"),
        P("group", None),
    )
    return jax.shard_map(
        per_device, mesh=mesh, in_specs=in_specs, out_specs=P("group", "tp"), check_vma=False
    )
```

```python
import functools

import jax
import jax.numpy as jnp
from jax import lax
from jax.experimental import pallas as pl
from jax.experimental.pallas import tpu as pltpu
from jax.sharding import PartitionSpec as P

MESH = pl.DeviceIdType.MESH
F32 = jnp.float32
BF16 = jnp.bfloat16
X_PARTS = 4


def kernel(
    n, groups, rank, tile,
    idr, idc, hid, res, w, a, b,
    out, xh, asib, bsib,
    hv, wv, pv, ring, av, xv, acc, ev, rv, dsend, drecv, mixb, rs, ag,
    ring_send, ring_recv, w_sem, a_sem, x_send, x_recv, sib_send, sib_recv,
    rs_send, rs_recv, ag_send, ag_recv, d_send, d_recv, loc, out_sem,
):
    rows, depth = hid.shape
    feats = res.shape[1]
    half = feats // 2
    a_rows = a.shape[0]
    tiles = a_rows // tile
    per_tile = tile // rank
    residents = a_rows // rank
    part = rows // X_PARTS
    sub = rows // 2
    block = 2 * rows // n
    blocks = n // 2

    t, g = lax.axis_index("tp"), lax.axis_index("group")
    z, y = t // 2, lax.rem(t, 2)
    pos = z + y * (n - 1 - 2 * z)

    def at(p):
        p = lax.rem(p + 2 * n, n)
        c = p // (n // 2)
        return 2 * p * (1 - c) + c * (2 * (n - 1 - p) + 1)

    toward = (at(pos + 1), at(pos - 1))
    across = lax.rem(g + groups // 2, groups)
    sibling = g + 1 - 2 * lax.rem(g, 2)

    barrier = pltpu.get_barrier_semaphore()
    for k in range(1, n):
        pl.semaphore_signal(
            barrier, inc=1, device_id=(g, lax.rem(t + k, n)), device_id_type=MESH
        )
    for other in (across, sibling):
        pl.semaphore_signal(barrier, inc=1, device_id=(other, t), device_id_type=MESH)

    own_copy = pltpu.make_async_copy(hid, hv, loc.at[0])
    own_copy.start()

    def w_copy(s, d):
        hops = n - 1 - s
        dest = at(pos + hops) if d == 0 else at(pos - hops)
        column = pl.multiple_of(dest * feats + d * half, half)
        return pltpu.make_async_copy(
            w.at[:, pl.ds(column, half)], wv.at[d, pl.ds(0, depth)], w_sem.at[d]
        )

    for d in range(2):
        w_copy(0, d).start()
    res_copy = pltpu.make_async_copy(res, rv, loc.at[1])
    res_copy.start()
    pl.semaphore_wait(barrier, n + 1)

    def x_copy(c):
        where = pl.ds(pl.multiple_of(c * part, part), part)
        return pltpu.make_async_remote_copy(
            src_ref=hid.at[where], dst_ref=xh.at[where],
            send_sem=x_send.at[c], recv_sem=x_recv.at[c],
            device_id=(across, t), device_id_type=MESH,
        )

    a_copy = pltpu.make_async_remote_copy(
        src_ref=a, dst_ref=asib, send_sem=sib_send.at[0], recv_sem=sib_recv.at[0],
        device_id=(sibling, t), device_id_type=MESH,
    )
    b_copy = pltpu.make_async_remote_copy(
        src_ref=b, dst_ref=bsib, send_sem=sib_send.at[1], recv_sem=sib_recv.at[1],
        device_id=(sibling, t), device_id_type=MESH,
    )
    x_copy(0).start()
    x_copy(1).start()
    a_copy.start()
    b_copy.start()
    acc[...] = jnp.zeros_like(acc)
    own_copy.wait()

    def partial(s, d):
        w_copy(s, d).wait()
        width = min(256, half)

        def columns(i, carry):
            where = pl.ds(pl.multiple_of(i * width, width), width)
            pv[d, :, where] = jnp.dot(
                hv[...], wv[d, pl.ds(0, depth), where], preferred_element_type=F32
            )
            return carry

        lax.fori_loop(0, half // width, columns, 0)

        @pl.when(s + 1 < n)
        def _():
            w_copy(s + 1, d).start()

    def adapter_of(i):
        theirs = i // tiles
        owner = g * (1 - theirs) + sibling * theirs
        return owner * residents + lax.rem(i, tiles) * per_tile

    def a_start(i, slot):
        @pl.when(i < tiles)
        def _():
            where = pl.ds(pl.multiple_of(lax.rem(i, tiles) * tile, tile), tile)
            pltpu.make_async_copy(a.at[where], av.at[slot], a_sem.at[slot]).start()

        @pl.when(i >= tiles)
        def _():
            where = pl.ds(pl.multiple_of(lax.rem(i, tiles) * tile, tile), tile)
            pltpu.make_async_copy(asib.at[where], av.at[slot], a_sem.at[slot]).start()

    def mix(first, count, rows_ref, column, width, ids_row):
        a_start(first, 0)

        def one(i, carry):
            @pl.when(i + 1 < count)
            def _():
                a_start(first + i + 1, lax.rem(i + 1, 2))

            slot = lax.rem(i, 2)
            pltpu.make_async_copy(
                a.at[pl.ds(0, tile)], av.at[slot], a_sem.at[slot]
            ).wait()
            products = lax.dot_general(
                av[slot], rows_ref[...], (((1,), (1,)), ((), ())),
                preferred_element_type=F32,
            )
            start = adapter_of(first + i)
            ids = idr[pl.ds(ids_row, 1), pl.ds(column, width)]
            where = pl.ds(pl.multiple_of(ids_row * rows + column, width), width)
            total = acc[:, where]
            for j in range(per_tile):
                total = total + jnp.where(
                    ids == start + j, products[j * rank:(j + 1) * rank], 0.0
                )
            acc[:, where] = total
            return carry

        lax.fori_loop(0, count, one, 0)

    def mix_across(c):
        x_copy(c).wait_recv()
        where = pl.ds(pl.multiple_of(c * part, part), part)
        copy = pltpu.make_async_copy(xh.at[where], xv, loc.at[2])
        copy.start()
        copy.wait()
        mix(0, 2 * tiles, xv, pl.multiple_of(c * part, part), part, 1)

    def ring_copy(s, d, h):
        where = pl.ds(h * sub, sub)
        return pltpu.make_async_remote_copy(
            src_ref=ring.at[d, s, where], dst_ref=ring.at[d, s + 1, where],
            send_sem=ring_send.at[d, s, h], recv_sem=ring_recv.at[d, s + 1, h],
            device_id=(g, toward[d]), device_id_type=MESH,
        )

    per_turn = 2 * tiles // X_PARTS

    def step(s, carry):
        for d in range(2):
            partial(s, d)

            @pl.when(s == 0)
            def _():
                for h in range(2):
                    where = pl.ds(h * sub, sub)
                    ring[d, 0, where] = pv[d, where].astype(BF16)
                    ring_copy(s, d, h).start()

        turn = s // 2

        @pl.when((lax.rem(s, 2) == 1) & (turn < X_PARTS))
        def _():
            mix(turn * per_turn, per_turn, hv, 0, rows, 0)

        @pl.when((lax.rem(s, 2) == 0) & (turn >= 1) & (turn < X_PARTS))
        def _():
            @pl.when(turn == 1)
            def _():
                a_copy.wait_recv()

            mix_across(turn - 1)

            @pl.when(turn + 1 < X_PARTS)
            def _():
                x_copy(turn + 1).start()

        @pl.when(s > 0)
        def _():
            for h in range(2):
                where = pl.ds(h * sub, sub)
                for d in range(2):
                    ring_copy(s - 1, d, h).wait_recv()

                    @pl.when(s < n - 1)
                    def _():
                        ring[d, s, where] = (
                            ring[d, s, where].astype(F32) + pv[d, where]
                        ).astype(BF16)
                        ring_copy(s, d, h).start()

                    @pl.when(s == n - 1)
                    def _():
                        pv[d, where] = ring[d, s, where].astype(F32) + pv[d, where]

        return carry

    lax.fori_loop(0, n, step, 0)

    b_copy.wait_recv()
    b_copies = []
    for d in range(2):
        for i, source in enumerate((b, bsib)):
            b_copies.append(
                pltpu.make_async_copy(
                    source.at[:, pl.ds(d * half, half)],
                    wv.at[d, pl.ds(i * a_rows, a_rows)],
                    loc.at[3 + 2 * d + i],
                )
            )
    for copy in b_copies:
        copy.start()

    def slice_out(q):
        return pltpu.make_async_remote_copy(
            src_ref=mixb.at[q], dst_ref=rs.at[t],
            send_sem=rs_send.at[q], recv_sem=rs_recv.at[t],
            device_id=(g, q), device_id_type=MESH,
        )

    def slice_in(q):
        return pltpu.make_async_copy(mixb.at[q], rs.at[q], rs_recv.at[q])

    def sum_out(q):
        return pltpu.make_async_remote_copy(
            src_ref=ag.at[t], dst_ref=ag.at[t],
            send_sem=ag_send.at[q], recv_sem=ag_recv.at[t],
            device_id=(g, q), device_id_type=MESH,
        )

    def sum_in(q):
        return pltpu.make_async_copy(mixb.at[q], ag.at[q], ag_recv.at[q])

    def send_slices(first, last):
        for q in range(first, last):
            mixb[q] = acc[:, q * block:(q + 1) * block].astype(BF16)

            @pl.when(t != q)
            def _():
                slice_out(q).start()

    early = (2 * rows - part) // block
    send_slices(0, early)
    mix_across(X_PARTS - 1)
    send_slices(early, n)
    total = mixb[t].astype(F32)
    for k in range(1, n):
        q = lax.rem(t + k, n)
        slice_in(q).wait()
        total = total + rs[q].astype(F32)
    ag[t] = total.astype(BF16)
    for k in range(1, n):
        sum_out(lax.rem(t + k, n)).start()
    for k in range(1, n):
        sum_in(lax.rem(t + k, n)).wait()
    for copy in b_copies:
        copy.wait()

    def delta(q, d_write):
        mixes = ag[q].astype(F32)
        wide = jnp.concatenate([mixes] * per_tile, axis=0).T.astype(BF16)
        ids = idc[pl.ds(pl.multiple_of(q * block, block), block), :]
        lane = lax.broadcasted_iota(jnp.int32, (block, tile), 1) // rank
        for i in range(2 * tiles):
            owner = g if i < tiles else sibling
            start = owner * residents + (i % tiles) * per_tile
            ev[:, i * tile:(i + 1) * tile] = jnp.where(
                ids == start + lane, wide, jnp.zeros_like(wide)
            )
        for d in range(2):
            d_write(
                d,
                jnp.dot(
                    ev[...], wv[d, pl.ds(0, 2 * a_rows)], preferred_element_type=F32
                ).astype(BF16),
            )

    def delta_copy(j):
        return pltpu.make_async_remote_copy(
            src_ref=dsend.at[j], dst_ref=drecv.at[j],
            send_sem=d_send.at[j], recv_sem=d_recv.at[j],
            device_id=(across, t), device_id_type=MESH,
        )

    def across_block(j, carry):
        def write(d, value):
            dsend[j, :, d * half:(d + 1) * half] = value

        delta(blocks + j, write)
        delta_copy(j).start()
        return carry

    lax.fori_loop(0, blocks, across_block, 0)
    res_copy.wait()

    def own_block(j, carry):
        where = pl.ds(pl.multiple_of(j * block, block), block)

        def write(d, value):
            pv[d, where] = pv[d, where] + value.astype(F32)

        delta(j, write)
        return carry

    lax.fori_loop(0, blocks, own_block, 0)

    def out_copy(j):
        where = pl.ds(pl.multiple_of(j * block, block), block)
        return pltpu.make_async_copy(rv.at[where], out.at[where], out_sem.at[j])

    def finish(j, carry):
        where = pl.ds(pl.multiple_of(j * block, block), block)
        delta_copy(j).wait_recv()
        for d in range(2):
            columns = slice(d * half, (d + 1) * half)
            rv[where, columns] = (
                rv[where, columns].astype(F32)
                + (pv[d, where] + drecv[j, :, columns].astype(F32))
            ).astype(BF16)
        out_copy(j).start()
        return carry

    lax.fori_loop(0, blocks, finish, 0)

    def drain(s, carry):
        for d in range(2):
            for h in range(2):
                ring_copy(s, d, h).wait_send()
        return carry

    lax.fori_loop(0, n - 1, drain, 0)
    for c in range(X_PARTS):
        x_copy(c).wait_send()
    a_copy.wait_send()
    b_copy.wait_send()
    for k in range(1, n):
        q = lax.rem(t + k, n)
        slice_out(q).wait_send()
        sum_out(q).wait_send()
    for j in range(blocks):
        delta_copy(j).wait_send()
        out_copy(j).wait()


def per_device(
    hidden, residual, down_projection_weight, adapter_down_maps, adapter_up_maps, row_adapter_index
):
    n, groups = lax.axis_size("tp"), lax.axis_size("group")
    rows, depth = hidden.shape
    feats = residual.shape[1]
    half = feats // 2
    residents, rank, _ = adapter_down_maps.shape
    a_rows = residents * rank
    tile = 8 * rank
    block, blocks = 2 * rows // n, n // 2
    ids = row_adapter_index[:, 0]
    swap = [(i, (i + groups // 2) % groups) for i in range(groups)]
    both = jnp.stack([ids, lax.ppermute(ids, "group", swap)])
    hbm = pl.BlockSpec(memory_space=pl.ANY)
    vmem = pl.BlockSpec(memory_space=pltpu.VMEM)
    dma = pltpu.SemaphoreType.DMA
    bf16 = functools.partial(jax.ShapeDtypeStruct, dtype=BF16)
    outs = pl.pallas_call(
        functools.partial(kernel, n, groups, rank, tile),
        out_shape=[
            bf16((rows, feats)), bf16((rows, depth)),
            bf16((a_rows, depth)), bf16((a_rows, feats)),
        ],
        in_specs=[vmem, vmem, hbm, hbm, hbm, hbm, hbm],
        out_specs=[hbm] * 4,
        scratch_shapes=[
            pltpu.VMEM((rows, depth), BF16),
            pltpu.VMEM((2, max(depth, 2 * a_rows), half), BF16),
            pltpu.VMEM((2, rows, half), F32),
            pltpu.VMEM((2, n, rows, half), BF16),
            pltpu.VMEM((2, tile, depth), BF16),
            pltpu.VMEM((rows // X_PARTS, depth), BF16),
            pltpu.VMEM((rank, 2 * rows), F32),
            pltpu.VMEM((block, 2 * a_rows), BF16),
            pltpu.VMEM((rows, feats), BF16),
            pltpu.VMEM((blocks, block, feats), BF16),
            pltpu.VMEM((blocks, block, feats), BF16),
            pltpu.VMEM((n, rank, block), BF16),
            pltpu.VMEM((n, rank, block), BF16),
            pltpu.VMEM((n, rank, block), BF16),
            dma((2, n, 2)), dma((2, n, 2)), dma((2,)), dma((2,)),
            dma((X_PARTS,)), dma((X_PARTS,)), dma((2,)), dma((2,)),
            dma((n,)), dma((n,)), dma((n,)), dma((n,)),
            dma((blocks,)), dma((blocks,)), dma((7,)), dma((blocks,)),
        ],
        compiler_params=pltpu.CompilerParams(
            collective_id=0, has_side_effects=True, vmem_limit_bytes=62 * 2**20
        ),
        cost_estimate=pl.CostEstimate(
            flops=2 * rows * depth * (n * feats + 4 * a_rows),
            bytes_accessed=2 * depth * n * feats,
            transcendentals=0,
        ),
        name="ring_and_adapters",
    )(
        both, both.reshape(2 * rows, 1), hidden, residual, down_projection_weight,
        adapter_down_maps.reshape(a_rows, depth), adapter_up_maps.reshape(a_rows, feats),
    )
    return outs[0]


def solution(mesh):
    in_specs = (
        P("group", "tp"),
        P("group", "tp"),
        P("tp", None),
        P("group", None, "tp"),
        P("group", None, "tp"),
        P("group", None),
    )
    return jax.shard_map(
        per_device, mesh=mesh, in_specs=in_specs, out_specs=P("group", "tp"), check_vma=False
    )
```
